256 devices in a mesh: row: 8 (over y_lo, x), col: 32 (over y_hi, z, core).
Axes of the slice: x: 4, y: 4 (y_hi: 2, y_lo: 2; y = y_hi * 2 + y_lo), z: 8, core: 2. Of those that a mesh axis runs over, the one named last changes fastest.
Arguments:
- cov: bfloat16 [16384, 16384], P('row', 'col'), as said below
- jac_blocks: bfloat16 [256, 128, 128], P('col'), may hold values from -0.25 to 0.25
- block_positions: int32 [256, 2], P('col'), may hold values from 0 to 127, as said below
- block_counts: int32 [32], P('col'), may hold values from 1 to 8, as said below
- lower_cross_block: float32 [512, 512], replicated, may hold values from -0.25 to 0.25
- pivot_inverse: float32 [2, 512, 512], replicated, as said below
Outputs:
- updated_cov: bfloat16 [16384, 16384], P('row', 'col')
The draws below stay inside these ranges and needn't reach their ends.
Inputs may be any that keep to these rules, and one draw needn't show every extreme that they name: `block_positions`: block coordinates: column 0 is a measurement block below 8, column 1 a cell block that belongs to the slot's own index of col (slots of index c hold cell blocks c * 4 to (c + 1) * 4 - 1); no pair repeats among the live slots. `block_counts`: some index of col holds exactly 8 live blocks. `cov`: Symmetric. `pivot_inverse`: Symmetric.
All inputs are finite; a program needn't handle non-finite values.
Results may differ from the reference program's by a relative error of at most 0.0063.
Values may be sent and summed in bfloat16 or wider, within the bound.
A program may use at most 128 MiB of HBM per device.

```python
import math
import jax
import jax.numpy as jnp
from jax import lax

BS = 128
PANEL = 512
BCAP = 8
WINDOW_CELLS = 16384
MEASUREMENT_COUNT = 1024
MB = 8
CB_COL = 4
BLOCKS = 256
N_ROW = 8
N_COL = 32


def draw_cov(key, part):
    key = jax.random.fold_in(key, 1)
    first, second = jax.random.split(key, 2)
    raw = jax.random.normal(first, (WINDOW_CELLS, WINDOW_CELLS), jnp.float32)
    symmetric = (raw + raw.T) * (0.7 / math.sqrt(WINDOW_CELLS))
    diagonal = jnp.exp(jax.random.uniform(second, (WINDOW_CELLS,), jnp.float32, math.log(0.5), math.log(2.0)))
    index = jnp.arange(WINDOW_CELLS)
    full = jnp.where(index[:, None] == index[None, :], diagonal[:, None], symmetric)
    return full.astype(jnp.bfloat16)


def draw_block_positions(key, part):
    key = jax.random.fold_in(key, 2)
    device_keys = jax.random.split(key, N_COL)
    chosen = jax.vmap(lambda one: jax.random.permutation(one, MB * CB_COL))(device_keys)[:, :BCAP]
    block_of_rows = chosen // CB_COL
    cell_block = jnp.arange(N_COL, dtype=jnp.int32)[:, None] * CB_COL + chosen % CB_COL
    return jnp.stack([block_of_rows, cell_block], axis=2).reshape(BLOCKS, 2).astype(jnp.int32)


def draw_block_counts(key, part):
    key = jax.random.fold_in(key, 3)
    first, second = jax.random.split(key)
    counts = jax.random.randint(first, (N_COL,), max(1, BCAP // 4), BCAP + 1)
    fullest = jax.random.randint(second, (), 0, N_COL)
    return jnp.where(jnp.arange(N_COL) == fullest, BCAP, counts).astype(jnp.int32)


def draw_pivot_inverse(key, part):
    key = jax.random.fold_in(key, 4)
    first, second = jax.random.split(key)
    diagonal = jnp.exp(jax.random.uniform(first, (2, PANEL), jnp.float32, math.log(0.3), math.log(1.0)))
    raw = jax.random.normal(second, (2, PANEL, PANEL), jnp.float32)
    coupling = 0.32
    root = jnp.sqrt(diagonal)
    symmetric = (raw + jnp.swapaxes(raw, 1, 2)) * (coupling / math.sqrt(PANEL))
    symmetric = symmetric * (root[:, :, None] * root[:, None, :])
    index = jnp.arange(PANEL)
    eye = index[:, None] == index[None, :]
    return jnp.where(eye[None], diagonal[:, :, None], symmetric).astype(jnp.float32)


def levels(rng, dims, pieces, least, high):
    def one(position, blocks):
        steps = jax.random.uniform(jax.random.fold_in(jax.random.fold_in(rng, 6), position), (blocks,), jnp.float32, least / len(pieces), high / len(pieces))
        return jnp.repeat(jnp.exp(steps), dims[position] // blocks).reshape((-1,) + (1,) * (len(dims) - position - 1))

    loudness = one(*pieces[0])
    for cut in pieces[1:]:
        loudness = loudness * one(*cut)
    return loudness


def bell_draw(own_key, extent, width, reach, shards=(), kind=jnp.bfloat16):
    drawn = jax.random.normal(own_key, extent, jnp.float32) * width
    if len(shards) > 0:
        drawn = levels(own_key, extent, shards, -0.22, 0.18) * drawn
    return jnp.clip(drawn, min=-reach, max=reach).astype(kind)


def setup_inputs(seed: int = 0) -> dict:
    splits = jax.random.split(jax.random.key(seed), 7)
    cov = draw_cov(jax.random.fold_in(splits[6], 71), 0)
    jac_blocks = bell_draw(splits[1], (BLOCKS, BS, BS), (4 * BS) ** -0.5, 0.25, ((0, 32),))
    block_positions = draw_block_positions(jax.random.fold_in(splits[6], 71), 0)
    block_counts = draw_block_counts(jax.random.fold_in(splits[6], 71), 0)
    lower_cross_block = bell_draw(splits[4], (PANEL, PANEL), PANEL ** -0.5, 0.25, (), jnp.float32)
    pivot_inverse = draw_pivot_inverse(jax.random.fold_in(splits[6], 71), 0)
    return dict(cov=cov, jac_blocks=jac_blocks, block_positions=block_positions, block_counts=block_counts, lower_cross_block=lower_cross_block, pivot_inverse=pivot_inverse)


def assemble(jac_blocks, block_positions, block_counts):
    slots = jnp.arange(BLOCKS, dtype=jnp.int32)
    owners = slots // BCAP
    active_slots = (slots % BCAP) < block_counts[owners]
    block_of_rows = jnp.where(active_slots, block_positions[:, 0], MB).astype(jnp.int32)
    dense_matrix = jnp.zeros((MB + 1, WINDOW_CELLS // BS, BS, BS), jnp.float32)
    dense_matrix = dense_matrix.at[block_of_rows, block_positions[:, 1]].add(jac_blocks.astype(jnp.float32))[:MB]
    return dense_matrix.transpose(0, 2, 1, 3).reshape(MEASUREMENT_COUNT, WINDOW_CELLS).astype(jnp.bfloat16)


def panel_solve(values, lower_cross_block, pivot_inverse):
    highest = lax.Precision.HIGHEST
    first = values[:PANEL]
    second = values[PANEL:]
    reduced = second - jnp.dot(lower_cross_block, first, precision=highest)
    scaled_one = jnp.dot(pivot_inverse[0], first, precision=highest)
    scaled_two = jnp.dot(pivot_inverse[1], reduced, precision=highest)
    top = scaled_one - jnp.dot(lower_cross_block.T, scaled_two, precision=highest)
    return jnp.concatenate([top, scaled_two], axis=0)


def reference(cov, jac_blocks, block_positions, block_counts, lower_cross_block, pivot_inverse):
    jacobian = assemble(jac_blocks, block_positions, block_counts)
    innov_rows = jnp.dot(jacobian, cov, preferred_element_type=jnp.float32).astype(jnp.bfloat16)
    weighted_product = panel_solve(innov_rows.astype(jnp.float32), lower_cross_block, pivot_inverse).astype(jnp.bfloat16)
    rows_per_tile = WINDOW_CELLS // N_ROW
    cov_tiles = cov.reshape(N_ROW, rows_per_tile, WINDOW_CELLS)
    weight_panels = weighted_product.reshape(MEASUREMENT_COUNT, N_ROW, rows_per_tile).transpose(1, 0, 2)

    def one_tile(pair):
        tile, gains = pair
        covariance_delta = jnp.dot(gains.T, innov_rows, preferred_element_type=jnp.float32)
        return (tile.astype(jnp.float32) - covariance_delta).astype(jnp.bfloat16)

    return lax.map(one_tile, (cov_tiles, weight_panels)).reshape(WINDOW_CELLS, WINDOW_CELLS)
```

```python
import jax
import jax.numpy as jnp
from jax import lax
from jax.experimental import pallas as pl
from jax.experimental.pallas import tpu as pltpu
from jax.sharding import PartitionSpec as P

MESH = pl.DeviceIdType.MESH
F32 = jnp.float32
BF16 = jnp.bfloat16


def dot(a, b):
    return jnp.dot(a, b, preferred_element_type=F32)


def split(values):
    high = values.astype(BF16)
    return high, (values - high.astype(F32)).astype(BF16)


def kernel(
    jac, pos, cnt, cov_hbm, lower, pivot, out,
    cov, jz, tz, jr, tr, table, lhs, psend, pown, rbuf, yb, xt, xb, fac, wb,
    cov_sem, tab_sem,
    z_s, z_r, zt_s, zt_r, p_s, p_r, pt_s, pt_r, d_s, d_r, dt_s, dt_r,
    r_s, r_r, y_s, y_r, a_s, a_r, h_s, h_r, s_s, s_r, u_s, u_r, v_s, v_r,
):
    r = lax.axis_index("row")
    c = lax.axis_index("col")
    y = c // 16
    z = (c // 2) % 8
    q = c % 2
    yl = r // 4
    x = r % 4
    b = c // 4
    j = c % 4

    def col(y_, z_, q_):
        return (y_ * 8 + z_) * 2 + q_

    def remote(src, dst, ss, rs, dev):
        return pltpu.make_async_remote_copy(
            src_ref=src, dst_ref=dst, send_sem=ss, recv_sem=rs, device_id=dev, device_id_type=MESH
        )

    cov_copy = pltpu.make_async_copy(cov_hbm, cov, cov_sem)
    cov_copy.start()

    sub = lax.broadcasted_iota(jnp.int32, (8, 128), 0)
    lane = lax.broadcasted_iota(jnp.int32, (8, 128), 1)
    t = jnp.full((8, 128), 8, jnp.int32)
    for s in range(8):
        hit = (sub == pos[s, 0]) & (lane == pos[s, 1] - c * 4) & (s < cnt[0])
        t = jnp.where(hit, s, t)
    tz[z] = t
    jz[z] = jac[r]

    def z_copy(zz, i):
        return remote(jac.at[r], jz.at[z], z_s.at[i], z_r.at[z], (r, col(y, zz, q)))

    def zt_copy(zz, i):
        return remote(tz.at[z], tz.at[z], zt_s.at[i], zt_r.at[z], (r, col(y, zz, q)))

    @pl.loop(1, 8)
    def _(i):
        zz = lax.rem(z + i, 8)
        z_copy(zz, i).start()
        zt_copy(zz, i).start()

    jr[32] = jnp.zeros((128, 128), BF16)
    for n, value in enumerate((lower[...], lower[...].T, pivot[0], pivot[1])):
        high, low = split(value)
        fac[n, 0] = high
        fac[n, 1] = low

    @pl.loop(0, 4)
    def _(i):
        xx = lax.rem(z // 2 + i, 4)
        for h in range(2):
            zz = 2 * xx + h

            @pl.when(zz != z)
            def _():
                remote(jac.at[r], jz.at[zz], z_s.at[0], z_r.at[zz], (r, c)).wait_recv()
                remote(tz.at[zz], tz.at[zz], zt_s.at[0], zt_r.at[zz], (r, c)).wait_recv()

        to = 4 * y + xx
        for yy in range(2):
            here = (to == r) & (yy == y)

            @pl.when(jnp.logical_not(here))
            def _():
                remote(
                    jz.at[pl.ds(2 * xx, 2)], jr.at[pl.ds((q * 8 + r) * 2, 2)],
                    p_s.at[i * 2 + yy], p_r.at[r], (to, col(yy, z, q)),
                ).start()

            @pl.when(here)
            def _():
                jr[pl.ds((q * 8 + r) * 2, 2)] = jz[pl.ds(2 * xx, 2)]

        @pl.when(to == r)
        def _():
            tr[q] = tz[pl.ds(2 * xx, 2)]
            remote(tz.at[pl.ds(2 * xx, 2)], tr.at[q], pt_s, pt_r, (r, col(1 - y, z, q))).start()

    sib = (r, col(y, z, 1 - q))

    @pl.when(yl != y)
    def _():
        remote(tz.at[pl.ds(0, 2)], tr.at[q], pt_s, pt_r, (r, c)).wait_recv()

    dt = remote(tr.at[q], tr.at[q], dt_s, dt_r, sib)
    dt.start()

    def p_wait(k):
        remote(jz.at[pl.ds(0, 2)], jr.at[pl.ds((q * 8 + k) * 2, 2)], p_s.at[0], p_r.at[k], (r, c)).wait_recv()

    def d_copy(k, side):
        part = jr.at[pl.ds((side * 8 + k) * 2, 2)]
        return remote(part, part, d_s.at[k], d_r.at[k], sib)

    @pl.loop(0, 8)
    def _(i):
        k = lax.rem(r + i, 8)

        @pl.when(jnp.logical_not((k == r) & (yl == y)))
        def _():
            p_wait(k)

        d_copy(k, q).start()

    remote(tr.at[q], tr.at[1 - q], dt_s, dt_r, sib).wait_recv()
    tab_copy = pltpu.make_async_copy(tr, table, tab_sem)
    tab_copy.start()
    tab_copy.wait()

    @pl.loop(0, 8)
    def _(k):
        d_copy(k, 1 - q).wait_recv()

    cov_copy.wait()

    @pl.loop(0, 4)
    def _(i):
        g = lax.rem(r // 2 + 1 + i, 4)
        for h in range(2):
            k = 2 * g + h
            for bb in range(2):
                for qq in range(2):
                    for l in range(4):
                        at = table[qq, bb, k, l]
                        at = jnp.where(at < 8, (qq * 8 + at) * 2 + bb, 32)
                        place = ((2 * bb + qq) * 4 + l) * 128
                        lhs[pl.ds(h * 128, 128), pl.ds(place, 128)] = jr[at]
        part = dot(lhs[...], cov[...])
        for h in range(2):
            k = 2 * g + h

            @pl.when(k == r)
            def _():
                pown[...] = part[h * 128:(h + 1) * 128]

            @pl.when(k != r)
            def _():
                psend[k] = part[h * 128:(h + 1) * 128].astype(BF16)
                remote(psend.at[k], rbuf.at[r], r_s.at[k], r_r.at[r], (k, c)).start()

    @pl.loop(1, 8)
    def _(i):
        k = lax.rem(r + 8 - i, 8)
        remote(psend.at[0], rbuf.at[k], r_s.at[0], r_r.at[k], (r, c)).wait_recv()
        pown[...] += rbuf[k].astype(F32)

    mine = pown[...]
    yb[r] = mine.astype(BF16)
    xt[...] = mine.T.astype(BF16)

    def xi(yy, zz, qq):
        return (zz * 2 + qq) * 2 + yy

    strip = pl.ds(pl.multiple_of(r * 128, 128), 128)
    own = xi(y, z, q)

    @pl.loop(0, 8)
    def _(i_):
        i = lax.rem(r + i_, 8)
        cc = 4 * i + j
        at = xi(cc // 16, (cc // 2) % 8, cc % 2)
        here = (b == r) & (i == b)

        @pl.when(jnp.logical_not(here))
        def _():
            remote(
                xt.at[pl.ds(i * 64, 64)], xb.at[at, :, strip], a_s.at[i], a_r.at[r], (b, cc)
            ).start()

        @pl.when(here)
        def _():
            xb[at, :, strip] = xt[pl.ds(pl.multiple_of(i * 64, 64), 64), :]

    def y_copy(k):
        return remote(yb.at[r], yb.at[r], y_s.at[k], y_r.at[r], (k, c))

    @pl.loop(1, 8)
    def _(i):
        y_copy(lax.rem(r + i, 8)).start()

    @pl.loop(0, 8)
    def _(a):
        @pl.when(jnp.logical_not((a == r) & (r == b)))
        def _():
            remote(
                xt.at[pl.ds(0, 64)], xb.at[own, :, pl.ds(pl.multiple_of(a * 128, 128), 128)],
                a_s.at[0], a_r.at[a], (r, c),
            ).wait_recv()

    def h_copy():
        return remote(xb.at[own], xb.at[own], h_s, h_r, (r, col(1 - y, z, q)))

    def line(sub_):
        return y if sub_ == 0 else 1 - y

    def fwd(at, sems_s, sems_r, n, dev):
        return remote(xb.at[at], xb.at[at], sems_s.at[n], sems_r.at[n], dev)

    up = (r, col(y, lax.rem(z + 1, 8), q))
    down = (r, col(y, lax.rem(z + 7, 8), q))

    def spread(off, sub_, go_up, go_down):
        at = xi(line(sub_), lax.rem(z + off, 8), q)
        if go_up:
            fwd(at, u_s, u_r, ((8 - off) % 8) * 2 + sub_, up).start()
        if go_down:
            fwd(at, v_s, v_r, off * 2 + sub_, down).start()
        fwd(at, s_s, s_r, off * 2 + sub_, sib).start()

    h_copy().start()
    spread(0, 0, True, True)
    remote(xb.at[own], xb.at[xi(1 - y, z, q)], h_s, h_r, (r, c)).wait_recv()
    spread(0, 1, True, True)

    def limits(sub_):
        return 4 - sub_, 3 + sub_

    @pl.loop(1, 8)
    def _(i):
        k = lax.rem(r + 8 - i, 8)
        remote(yb.at[r], yb.at[k], y_s.at[0], y_r.at[k], (r, c)).wait_recv()

    def solve(half):
        cut = pl.ds(half * 256, 256)
        y1 = yb[pl.ds(0, 4), :, cut].reshape(512, 256)
        y2 = yb[pl.ds(4, 4), :, cut].reshape(512, 256)
        z2 = y2.astype(F32) - (dot(fac[0, 0], y1) + dot(fac[0, 1], y1))
        zh, zl = split(z2)
        w1 = dot(fac[2, 0], y1) + dot(fac[2, 1], y1)
        w2 = dot(fac[3, 0], zh) + dot(fac[3, 1], zh) + dot(fac[3, 0], zl)
        wh, wl = split(w2)
        top = w1 - (dot(fac[1, 0], wh) + dot(fac[1, 1], wh) + dot(fac[1, 0], wl))
        wb[pl.ds(0, 512), cut] = top.astype(BF16)
        wb[pl.ds(512, 512), cut] = wh

    solve(0)
    solve(1)

    def finish(off):
        zz = lax.rem(z + off, 8)
        x4 = xb[pl.ds(zz * 4, 4)].reshape(256, 1024)
        delta = dot(x4, wb[...])
        for qq in range(2):
            for yy in range(2):
                row = ((zz % 2) * 2 + qq) * 512 + (yy * 4 + zz // 2) * 64
                rows = pl.ds(pl.multiple_of(row, 64), 64)
                n = (qq * 2 + yy) * 64
                out[rows, :] = (cov[rows, :].astype(F32) - delta[n:n + 64]).astype(BF16)

    def from_sibling(off):
        for sub_ in range(2):
            at = xi(line(sub_), lax.rem(z + off, 8), 1 - q)
            fwd(at, s_s, s_r, off * 2 + sub_, sib).wait_recv()

    from_sibling(0)
    finish(0)
    for d in range(1, 5):
        for sub_ in range(2):
            top_up, top_down = limits(sub_)
            if d <= top_up:
                at = xi(line(sub_), lax.rem(z + 8 - d, 8), q)
                fwd(at, u_s, u_r, (d - 1) * 2 + sub_, up).wait_recv()
                spread(8 - d, sub_, d < top_up, False)
            if d <= top_down:
                at = xi(line(sub_), lax.rem(z + d, 8), q)
                fwd(at, v_s, v_r, (d - 1) * 2 + sub_, down).wait_recv()
                spread(d, sub_, False, d < top_down)
        for off in ((8 - d, d) if d < 4 else (4,)):
            from_sibling(off)
            finish(off)

    @pl.loop(1, 8)
    def _(i):
        k = lax.rem(r + i, 8)
        z_copy(0, i).wait_send()
        zt_copy(0, i).wait_send()
        remote(psend.at[k], rbuf.at[r], r_s.at[k], r_r.at[r], (r, c)).wait_send()
        y_copy(k).wait_send()

    @pl.loop(0, 8)
    def _(i):
        to = 4 * y + lax.rem(z // 2 + i // 2, 4)

        @pl.when(jnp.logical_not((to == r) & (i % 2 == y)))
        def _():
            remote(
                jz.at[pl.ds(0, 2)], jr.at[pl.ds((q * 8 + r) * 2, 2)], p_s.at[i], p_r.at[r], (r, c)
            ).wait_send()

        d_copy(i, q).wait_send()

        @pl.when(jnp.logical_not((b == r) & (i == b)))
        def _():
            remote(xt.at[pl.ds(0, 64)], xb.at[own, :, strip], a_s.at[i], a_r.at[r], (r, c)).wait_send()

    @pl.when(yl == y)
    def _():
        remote(tz.at[pl.ds(0, 2)], tr.at[q], pt_s, pt_r, (r, c)).wait_send()

    dt.wait_send()
    h_copy().wait_send()

    @pl.loop(0, 16)
    def _(n):
        fwd(own, s_s, s_r, n, sib).wait_send()

    @pl.loop(0, 7)
    def _(n):
        fwd(own, u_s, u_r, n, up).wait_send()
        fwd(own, v_s, v_r, jnp.where(n == 6, 7, n), down).wait_send()


def body(cov, jac_blocks, block_positions, block_counts, lower_cross_block, pivot_inverse):
    dma = pltpu.SemaphoreType.DMA
    vmem = pltpu.VMEM
    v_spec = pl.BlockSpec(memory_space=pltpu.VMEM)
    s_spec = pl.BlockSpec(memory_space=pltpu.SMEM)
    return pl.pallas_call(
        kernel,
        out_shape=jax.ShapeDtypeStruct(cov.shape, cov.dtype),
        in_specs=[v_spec, s_spec, s_spec, pl.BlockSpec(memory_space=pl.ANY), v_spec, v_spec],
        out_specs=v_spec,
        scratch_shapes=[
            vmem((2048, 512), BF16),
            vmem((8, 128, 128), BF16),
            vmem((8, 8, 128), jnp.int32),
            vmem((33, 128, 128), BF16),
            vmem((2, 2, 8, 128), jnp.int32),
            pltpu.SMEM((2, 2, 8, 128), jnp.int32),
            vmem((256, 2048), BF16),
            vmem((8, 128, 512), BF16),
            vmem((128, 512), F32),
            vmem((8, 128, 512), BF16),
            vmem((8, 128, 512), BF16),
            vmem((512, 128), BF16),
            vmem((32, 64, 1024), BF16),
            vmem((4, 2, 512, 512), BF16),
            vmem((1024, 512), BF16),
            dma, dma,
            dma((8,)), dma((8,)), dma((8,)), dma((8,)),
            dma((8,)), dma((8,)), dma, dma,
            dma((8,)), dma((8,)), dma, dma,
            dma((8,)), dma((8,)), dma((8,)), dma((8,)),
            dma((8,)), dma((8,)), dma, dma,
            dma((16,)), dma((16,)),
            dma((8,)), dma((8,)), dma((8,)), dma((8,)),
        ],
        compiler_params=pltpu.CompilerParams(
            has_side_effects=True, vmem_limit_bytes=48 * 1024 * 1024
        ),
        cost_estimate=pl.CostEstimate(flops=9 * 2**30, bytes_accessed=8 * 2**20, transcendentals=0),
    )(jac_blocks, block_positions, block_counts, cov, lower_cross_block, pivot_inverse)


def solution(mesh):
    return jax.shard_map(
        body,
        mesh=mesh,
        in_specs=(P("row", "col"), P("col", None, None), P("col", None), P("col"), P(), P()),
        out_specs=P("row", "col"),
        check_vma=False,
    )
```

```python
import jax
import jax.numpy as jnp
from jax import lax
from jax.experimental import pallas as pl
from jax.experimental.pallas import tpu as pltpu
from jax.sharding import PartitionSpec as P

MESH = pl.DeviceIdType.MESH
F32 = jnp.float32
BF16 = jnp.bfloat16


def dot(a, b):
    return jnp.dot(a, b, preferred_element_type=F32)


def split(values):
    high = values.astype(BF16)
    return high, (values - high.astype(F32)).astype(BF16)


def kernel(
    jac, pos, cnt, cov_hbm, lower_hbm, pivot_hbm, out,
    cov, ob, lower, pivot, jz, tz, jr, tr, table, lhs, psend, pown, rbuf, yb, xt, xz, xb, fac, wb,
    cov_sem, low_sem, piv_sem, own_sem, tab_sem, out_sem,
    z_s, z_r, zt_s, zt_r, p_s, p_r, pt_s, pt_r, d_s, d_r, dt_s, dt_r,
    r_s, r_r, y_s, y_r, a_s, a_r, b_s, b_r, s_s, s_r, u_s, u_r, v_s, v_r,
):
    r = lax.axis_index("row")
    c = lax.axis_index("col")
    y = c // 16
    z = (c // 2) % 8
    q = c % 2
    yl = r // 4
    x = r % 4
    b = c // 4
    j = c % 4

    def col(y_, z_, q_):
        return (y_ * 8 + z_) * 2 + q_

    def remote(src, dst, ss, rs, dev):
        return pltpu.make_async_remote_copy(
            src_ref=src, dst_ref=dst, send_sem=ss, recv_sem=rs, device_id=dev, device_id_type=MESH
        )

    barrier = pltpu.get_barrier_semaphore()

    def ready(row, col_):
        pl.semaphore_signal(barrier, inc=1, device_id=(row, col_), device_id_type=MESH)

    @pl.loop(1, 8)
    def _(i):
        ready(r, col(y, lax.rem(z + i, 8), q))

    @pl.loop(1, 8)
    def _(i):
        ready(lax.rem(r + i, 8), c)

    @pl.when(yl != y)
    def _():
        @pl.loop(0, 8)
        def _(a):
            ready(a, col(1 - y, z, q))

    ready(r, col(y, z, 1 - q))

    low_copy = pltpu.make_async_copy(lower_hbm, lower, low_sem)
    piv_copy = pltpu.make_async_copy(pivot_hbm, pivot, piv_sem)
    cov_copy = pltpu.make_async_copy(cov_hbm, cov, cov_sem)
    own_copy = pltpu.make_async_copy(jac.at[r], jz.at[z], own_sem)
    own_copy.start()
    low_copy.start()
    piv_copy.start()
    cov_copy.start()

    sub = lax.broadcasted_iota(jnp.int32, (8, 128), 0)
    lane = lax.broadcasted_iota(jnp.int32, (8, 128), 1)
    t = jnp.full((8, 128), 8, jnp.int32)
    for s in range(8):
        hit = (sub == pos[0, s]) & (lane == pos[1, s] - c * 4) & (s < cnt[0])
        t = jnp.where(hit, s, t)
    tz[z] = t
    pl.semaphore_wait(barrier, 19)

    def z_copy(zz, i):
        return remote(jac.at[r], jz.at[z], z_s.at[i], z_r.at[z], (r, col(y, zz, q)))

    def zt_copy(zz, i):
        return remote(tz.at[z], tz.at[z], zt_s.at[i], zt_r.at[z], (r, col(y, zz, q)))

    tables = (yl == y) & (z // 2 == x)

    def near(i):
        return jnp.where(i % 2 == 1, (i + 1) // 2, 8 - i // 2)

    @pl.loop(1, 8)
    def _(i):
        zz = lax.rem(z + near(i), 8)
        z_copy(zz, i).start()

        @pl.when(tables)
        def _():
            zt_copy(zz, i).start()

    jr[32] = jnp.zeros((128, 128), BF16)
    own_copy.wait()

    def p_copy(i, yy, k, zz, dev):
        return remote(
            jz.at[zz], jr.at[(q * 8 + k) * 2 + zz % 2], p_s.at[i, yy], p_r.at[k, zz % 2], dev
        )

    @pl.loop(0, 8)
    def _(i):
        zz = lax.rem(z + jnp.where(i == 0, 0, near(i)), 8)
        to = 4 * y + zz // 2

        @pl.when(i != 0)
        def _():
            remote(jac.at[r], jz.at[zz], z_s.at[0], z_r.at[zz], (r, c)).wait_recv()

            @pl.when(to == r)
            def _():
                remote(tz.at[zz], tz.at[zz], zt_s.at[0], zt_r.at[zz], (r, c)).wait_recv()

        @pl.when(jnp.logical_not((to == r) & (y == 0)))
        def _():
            p_copy(i, 0, r, zz, (to, col(0, z, q))).start()

        @pl.when(jnp.logical_not((to == r) & (y == 1)))
        def _():
            p_copy(i, 1, r, zz, (to, col(1, z, q))).start()

        @pl.when(to == r)
        def _():
            jr[(q * 8 + r) * 2 + zz % 2] = jz[zz]
            tr[q, zz % 2] = tz[zz]

    def pt_copy():
        return remote(
            tr.at[q], tr.at[q], pt_s, pt_r, (r, col(1 - y, z, q))
        )

    @pl.when(yl == y)
    def _():
        pt_copy().start()

    low_copy.wait()
    piv_copy.wait()
    for n, value in enumerate((lower[...], lower[...].T, pivot[0], pivot[1])):
        high, low = split(value)
        fac[n, 0] = high
        fac[n, 1] = low

    sib = (r, col(y, z, 1 - q))

    @pl.when(yl != y)
    def _():
        pt_copy().wait_recv()

    dt = remote(tr.at[q], tr.at[q], dt_s, dt_r, sib)
    dt.start()

    def d_copy(k, side):
        part = jr.at[pl.ds((side * 8 + k) * 2, 2)]
        return remote(part, part, d_s.at[k], d_r.at[k], sib)

    @pl.loop(0, 8)
    def _(i):
        k = lax.rem(r + i, 8)

        @pl.when(jnp.logical_not((k == r) & (yl == y)))
        def _():
            p_copy(0, 0, k, 0, (r, c)).wait_recv()
            p_copy(0, 0, k, 1, (r, c)).wait_recv()

        d_copy(k, q).start()

    remote(tr.at[q], tr.at[1 - q], dt_s, dt_r, sib).wait_recv()
    tab_copy = pltpu.make_async_copy(tr, table, tab_sem)
    tab_copy.start()
    tab_copy.wait()

    @pl.loop(0, 8)
    def _(k):
        d_copy(k, 1 - q).wait_recv()


    @pl.loop(0, 8)
    def _(k):
        for bb in range(2):
            for qq in range(2):
                for l in range(4):
                    at = table[qq, bb, k, l]
                    at = jnp.where(at < 8, (qq * 8 + at) * 2 + bb, 32)
                    place = ((2 * bb + qq) * 4 + l) * 128
                    lhs[k, :, place:place + 128] = jr[at]

    cov_copy.wait()

    for g in range(2):

        @pl.loop(0, 4)
        def _(i):
            pair = lax.rem(r // 2 + 1 + i, 4)
            part = dot(
                lhs[pl.ds(2 * pair, 2)].reshape(256, 2048), cov[:, g * 256:(g + 1) * 256]
            )
            for h in range(2):
                k = 2 * pair + h

                @pl.when(k == r)
                def _():
                    pown[g] = part[h * 128:(h + 1) * 128]

                @pl.when(k != r)
                def _():
                    psend[g, k] = part[h * 128:(h + 1) * 128].astype(BF16)
                    remote(
                        psend.at[g, k], rbuf.at[g, r], r_s.at[g, k], r_r.at[g, r], (k, c)
                    ).start()


    def block(zz, qq):
        return pl.ds((lax.rem(zz, 4) * 2 + qq) * 4, 4)

    def half(zz, qq, yy):
        return pl.ds(((lax.rem(zz, 4) * 2 + qq) * 2 + yy) * 2, 2)

    def strip(a):
        return pl.ds(pl.multiple_of(a * 128, 128), 128)

    def a_copy(g, i, dev):
        return remote(
            xt.at[g, lax.rem(i, 2)], xz.at[g, z // 2], a_s.at[g, i], a_r.at[g, z // 2], dev
        )

    def b_copy(g, n, yy, dev):
        return remote(
            xz.at[g, n], xb.at[g, block(z, q), :, strip(r)],
            b_s.at[g, n, yy], b_r.at[g, r], dev,
        )

    def y_copy(g, k):
        return remote(yb.at[g, r], yb.at[g, r], y_s.at[g, k], y_r.at[g, r], (k, c))

    def total(g):
        @pl.loop(1, 8)
        def _(i):
            k = lax.rem(r + 8 - i, 8)
            remote(psend.at[g, 0], rbuf.at[g, k], r_s.at[g, 0], r_r.at[g, k], (r, c)).wait_recv()
            pown[g] += rbuf[g, k].astype(F32)

        mine = pown[g]
        yb[g, r] = mine.astype(BF16)
        turned = mine.T.astype(BF16).reshape(2, 4, 32, 128)
        for i in range(4):
            for yy in range(2):
                xt[g, i % 2, yy * 2 + i // 2] = turned[yy, i]
        xz[g, z // 2] = xt[g, (z // 2) % 2]

        for n in range(1, 4):
            i = lax.rem(z // 2 + n, 4)
            a_copy(g, i, (r, col(y, i * 2 + z % 2, q))).start()

    def turn(g):
        for n_ in range(4):
            n = lax.rem(z // 2 + (0, 1, 3, 2)[n_], 4)
            if n_ > 0:
                remote(xt.at[g, 0], xz.at[g, n], a_s.at[g, 0], a_r.at[g, n], (r, c)).wait_recv()
            to = 4 * y + n
            for yy in range(2):
                here = (to == r) & (yy == y)

                @pl.when(jnp.logical_not(here))
                def _():
                    b_copy(g, n, yy, (to, col(yy, z, q))).start()

                @pl.when(here)
                def _():
                    xb[g, block(z, q), :, strip(r)] = xz[g, n]

    def to_rows(g):
        @pl.loop(1, 8)
        def _(i):
            y_copy(g, lax.rem(r + i, 8)).start()

    def fwd(g, zz, qq, yy, sems_s, sems_r, n, dev):
        part = xb.at[g, half(zz, qq, yy)]
        return remote(part, part, sems_s.at[g, n], sems_r.at[g, n], dev)

    up = (r, col(y, lax.rem(z + 1, 8), q))
    down = (r, col(y, lax.rem(z + 7, 8), q))

    def go_up(g, d, yy):
        return fwd(g, z + 4 - d, q, yy, u_s, u_r, d * 2 + yy, up)

    def go_down(g, d, yy):
        return fwd(g, z + d, q, yy, v_s, v_r, d * 2 + yy, down)

    def over(g, d, yy, qq):
        return fwd(g, z + d, qq, yy, s_s, s_r, d * 2 + yy, sib)

    def held(g):
        @pl.loop(0, 8)
        def _(a):
            @pl.when(jnp.logical_not((a == r) & (yl == y)))
            def _():
                remote(
                    xz.at[g, 0], xb.at[g, block(z, q), :, strip(a)],
                    b_s.at[g, 0, 0], b_r.at[g, a], (r, c),
                ).wait_recv()

        go_up(g, 0, 0).start()
        go_down(g, 0, 1).start()
        go_up(g, 0, 1).start()
        go_down(g, 0, 0).start()
        over(g, 0, 0, q).start()
        over(g, 0, 1, q).start()

    def came_up(g, d, yy):
        fwd(g, z + 4 - d, q, yy, u_s, u_r, (d - 1) * 2 + yy, up).wait_recv()

    def came_down(g, d, yy):
        fwd(g, z + d, q, yy, v_s, v_r, (d - 1) * 2 + yy, down).wait_recv()

    def ring1(g):
        came_up(g, 1, 0)
        go_up(g, 1, 0).start()
        over(g, 3, 0, q).start()
        came_down(g, 1, 1)
        go_down(g, 1, 1).start()
        over(g, 1, 1, q).start()

    def ring2(g):
        came_up(g, 1, 1)
        over(g, 3, 1, q).start()
        came_down(g, 1, 0)
        over(g, 1, 0, q).start()

    def ring3(g):
        came_up(g, 2, 0)
        over(g, 2, 0, q).start()
        came_down(g, 2, 1)
        over(g, 2, 1, q).start()

    def solve(g):
        @pl.loop(1, 8)
        def _(i):
            k = lax.rem(r + 8 - i, 8)
            remote(yb.at[g, r], yb.at[g, k], y_s.at[g, 0], y_r.at[g, k], (r, c)).wait_recv()

        cut = pl.ds(g * 256, 256)
        y1 = yb[g, 0:4].reshape(512, 256)
        y2 = yb[g, 4:8].reshape(512, 256)
        z2 = y2.astype(F32) - (dot(fac[0, 0], y1) + dot(fac[0, 1], y1))
        zh, zl = split(z2)
        w1 = dot(fac[2, 0], y1) + dot(fac[2, 1], y1)
        w2 = dot(fac[3, 0], zh) + dot(fac[3, 1], zh) + dot(fac[3, 0], zl)
        wh, wl = split(w2)
        top = w1 - (dot(fac[1, 0], wh) + dot(fac[1, 1], wh) + dot(fac[1, 0], wl))
        wb[pl.ds(0, 512), cut] = top.astype(BF16)
        wb[pl.ds(512, 512), cut] = wh

    def finish(g, off):
        for yy in range(2):
            over(g, off, yy, 1 - q).wait_recv()

        zz = lax.rem(z + off, 4)
        x8 = xb[g, pl.ds(zz * 8, 8)].reshape(256, 1024)
        delta = dot(x8, wb[...])
        for qq in range(2):
            for yy in range(2):
                for m in range(2):
                    row = ((zz % 2) * 2 + qq) * 512 + g * 256 + (yy * 4 + m * 2 + zz // 2) * 32
                    rows = pl.ds(pl.multiple_of(row, 32), 32)
                    n = ((qq * 2 + yy) * 2 + m) * 32
                    ob[rows, :] = (cov[rows, :].astype(F32) - delta[n:n + 32]).astype(BF16)

    def out_copy(g, n):
        rows = pl.ds(n * 512 + g * 256, 256)
        return pltpu.make_async_copy(ob.at[rows], out.at[rows], out_sem.at[g, n])

    def store(g):
        for n in range(4):
            out_copy(g, n).start()

    total(0)
    turn(0)
    total(1)
    held(0)
    turn(1)
    to_rows(0)
    to_rows(1)
    ring1(0)
    held(1)
    ring2(0)
    ring3(0)
    ring1(1)
    solve(0)
    ring2(1)
    solve(1)
    for off in range(4):
        finish(0, off)
    store(0)
    finish(1, 0)
    ring3(1)
    for off in (1, 3, 2):
        finish(1, off)
    store(1)

    @pl.loop(1, 8)
    def _(i):
        z_copy(0, i).wait_send()

        @pl.when(tables)
        def _():
            zt_copy(0, i).wait_send()

    for g in range(2):

        @pl.loop(1, 8)
        def _(i):
            k = lax.rem(r + i, 8)
            remote(psend.at[g, k], rbuf.at[g, r], r_s.at[g, k], r_r.at[g, r], (r, c)).wait_send()
            y_copy(g, k).wait_send()

        for n in range(1, 4):
            a_copy(g, lax.rem(z // 2 + n, 4), (r, c)).wait_send()

        @pl.loop(0, 4)
        def _(n):
            for yy in range(2):

                @pl.when(jnp.logical_not((4 * y + n == r) & (yy == y)))
                def _():
                    b_copy(g, n, yy, (r, c)).wait_send()

        for d in range(4):
            for yy in range(2):
                over(g, d, yy, q).wait_send()
        for d, yy in ((0, 0), (0, 1), (1, 0)):
            go_up(g, d, yy).wait_send()
            go_down(g, d, yy if d == 0 else 1).wait_send()

        for n in range(4):
            out_copy(g, n).wait()

    @pl.loop(0, 8)
    def _(i):
        zz = lax.rem(z + jnp.where(i == 0, 0, near(i)), 8)
        for yy in range(2):

            @pl.when(jnp.logical_not((4 * y + zz // 2 == r) & (y == yy)))
            def _():
                p_copy(i, yy, r, zz, (r, c)).wait_send()

        d_copy(i, q).wait_send()

    @pl.when(yl == y)
    def _():
        pt_copy().wait_send()

    dt.wait_send()


def body(cov, jac_blocks, block_positions, block_counts, lower_cross_block, pivot_inverse):
    dma = pltpu.SemaphoreType.DMA
    vmem = pltpu.VMEM
    h_spec = pl.BlockSpec(memory_space=pltpu.HBM)
    a_spec = pl.BlockSpec(memory_space=pl.ANY)
    s_spec = pl.BlockSpec(memory_space=pltpu.SMEM)
    return pl.pallas_call(
        kernel,
        out_shape=jax.ShapeDtypeStruct(cov.shape, cov.dtype),
        in_specs=[h_spec, s_spec, s_spec, h_spec, h_spec, h_spec],
        out_specs=a_spec,
        scratch_shapes=[
            vmem((2048, 512), BF16),
            vmem((2048, 512), BF16),
            vmem((512, 512), F32),
            vmem((2, 512, 512), F32),
            vmem((8, 128, 128), BF16),
            vmem((8, 8, 128), jnp.int32),
            vmem((33, 128, 128), BF16),
            vmem((2, 2, 8, 128), jnp.int32),
            pltpu.SMEM((2, 2, 8, 128), jnp.int32),
            vmem((8, 128, 2048), BF16),
            vmem((2, 8, 128, 256), BF16),
            vmem((2, 128, 256), F32),
            vmem((2, 8, 128, 256), BF16),
            vmem((2, 8, 128, 256), BF16),
            vmem((2, 2, 4, 32, 128), BF16),
            vmem((2, 4, 4, 32, 128), BF16),
            vmem((2, 32, 32, 1024), BF16),
            vmem((4, 2, 512, 512), BF16),
            vmem((1024, 512), BF16),
            dma, dma, dma, dma, dma, dma((2, 4)),
            dma((8,)), dma((8,)), dma((8,)), dma((8,)),
            dma((8, 2)), dma((8, 2)), dma, dma,
            dma((8,)), dma((8,)), dma, dma,
            dma((2, 8)), dma((2, 8)), dma((2, 8)), dma((2, 8)),
            dma((2, 4)), dma((2, 4)), dma((2, 4, 2)), dma((2, 8)),
            dma((2, 8)), dma((2, 8)),
            dma((2, 4)), dma((2, 4)), dma((2, 4)), dma((2, 4)),
        ],
        compiler_params=pltpu.CompilerParams(
            collective_id=0, has_side_effects=True, vmem_limit_bytes=62 * 1024 * 1024
        ),
        cost_estimate=pl.CostEstimate(flops=9 * 2**30, bytes_accessed=8 * 2**20, transcendentals=0),
    )(jac_blocks, block_positions.T, block_counts, cov, lower_cross_block, pivot_inverse)


def solution(mesh):
    return jax.shard_map(
        body,
        mesh=mesh,
        in_specs=(P("row", "col"), P("col", None, None), P("col", None), P("col"), P(), P()),
        out_specs=P("row", "col"),
        check_vma=False,
    )
```

```python
import jax
import jax.numpy as jnp
from jax import lax
from jax.experimental import pallas as pl
from jax.experimental.pallas import tpu as pltpu
from jax.sharding import PartitionSpec as P

MESH = pl.DeviceIdType.MESH
F32 = jnp.float32
BF16 = jnp.bfloat16


def dot(a, b):
    return jnp.dot(a, b, preferred_element_type=F32)


def split(values):
    high = values.astype(BF16)
    return high, (values - high.astype(F32)).astype(BF16)


def kernel(
    jac, pos, cnt, cov_hbm, lower_hbm, pivot_hbm, out,
    cov, ob, lower, pivot, jz, tz, jr, tr, table, lhs, psend, pown, rbuf, yb, xt, xz, xb, fac, wb,
    cov_sem, low_sem, piv_sem, own_sem, tab_sem, out_sem,
    z_s, z_r, zt_s, zt_r, p_s, p_r, pt_s, pt_r, d_s, d_r, dt_s, dt_r,
    r_s, r_r, y_s, y_r, a_s, a_r, b_s, b_r, s_s, s_r, u_s, u_r, v_s, v_r,
):
    r = lax.axis_index("row")
    c = lax.axis_index("col")
    y = c // 16
    z = (c // 2) % 8
    q = c % 2
    yl = r // 4
    x = r % 4
    b = c // 4
    j = c % 4

    def col(y_, z_, q_):
        return (y_ * 8 + z_) * 2 + q_

    def remote(src, dst, ss, rs, dev):
        return pltpu.make_async_remote_copy(
            src_ref=src, dst_ref=dst, send_sem=ss, recv_sem=rs, device_id=dev, device_id_type=MESH
        )

    low_copy = pltpu.make_async_copy(lower_hbm, lower, low_sem)
    piv_copy = pltpu.make_async_copy(pivot_hbm, pivot, piv_sem)
    cov_copy = pltpu.make_async_copy(cov_hbm, cov, cov_sem)
    own_copy = pltpu.make_async_copy(jac.at[r], jz.at[z], own_sem)
    own_copy.start()
    low_copy.start()
    piv_copy.start()
    cov_copy.start()

    barrier = pltpu.get_barrier_semaphore()

    def ready(row, col_):
        pl.semaphore_signal(barrier, inc=1, device_id=(row, col_), device_id_type=MESH)

    @pl.loop(1, 8)
    def _(i):
        ready(r, col(y, lax.rem(z + i, 8), q))

    @pl.loop(0, 8)
    def _(a):
        @pl.when(jnp.logical_not((a == r) & (yl == y)))
        def _():
            ready(a, col(yl, z, q))

    ready(r, col(y, z, 1 - q))

    sub = lax.broadcasted_iota(jnp.int32, (8, 128), 0)
    lane = lax.broadcasted_iota(jnp.int32, (8, 128), 1)
    t = jnp.full((8, 128), 8, jnp.int32)
    for s in range(8):
        hit = (sub == pos[0, s]) & (lane == pos[1, s] - c * 4) & (s < cnt[0])
        t = jnp.where(hit, s, t)
    tz[z] = t
    pl.semaphore_wait(barrier, jnp.where(yl == y, 15, 16))

    def z_copy(zz, i):
        return remote(jac.at[r], jz.at[z], z_s.at[i], z_r.at[z], (r, col(y, zz, q)))

    def zt_copy(zz, i):
        return remote(tz.at[z], tz.at[z], zt_s.at[i], zt_r.at[z], (r, col(y, zz, q)))

    tables = (yl == y) & (z // 2 == x)

    def near(i):
        return jnp.where(i % 2 == 1, (i + 1) // 2, 8 - i // 2)

    @pl.loop(1, 8)
    def _(i):
        zz = lax.rem(z + near(i), 8)
        z_copy(zz, i).start()

        @pl.when(tables)
        def _():
            zt_copy(zz, i).start()

    jr[32] = jnp.zeros((128, 128), BF16)
    own_copy.wait()

    def p_copy(i, yy, k, zz, dev):
        return remote(
            jz.at[zz], jr.at[(q * 8 + k) * 2 + zz % 2], p_s.at[i, yy], p_r.at[k, zz % 2], dev
        )

    @pl.loop(0, 8)
    def _(i):
        zz = lax.rem(z + jnp.where(i == 0, 0, near(i)), 8)
        to = 4 * y + zz // 2

        @pl.when(i != 0)
        def _():
            remote(jac.at[r], jz.at[zz], z_s.at[0], z_r.at[zz], (r, c)).wait_recv()

            @pl.when(to == r)
            def _():
                remote(tz.at[zz], tz.at[zz], zt_s.at[0], zt_r.at[zz], (r, c)).wait_recv()

        @pl.when(jnp.logical_not((to == r) & (y == 0)))
        def _():
            p_copy(i, 0, r, zz, (to, col(0, z, q))).start()

        @pl.when(jnp.logical_not((to == r) & (y == 1)))
        def _():
            p_copy(i, 1, r, zz, (to, col(1, z, q))).start()

        @pl.when(to == r)
        def _():
            jr[(q * 8 + r) * 2 + zz % 2] = jz[zz]
            tr[q, zz % 2] = tz[zz]

    def pt_copy():
        return remote(
            tr.at[q], tr.at[q], pt_s, pt_r, (r, col(1 - y, z, q))
        )

    @pl.when(yl == y)
    def _():
        pt_copy().start()

    low_copy.wait()
    piv_copy.wait()
    for n, value in enumerate((lower[...], lower[...].T, pivot[0], pivot[1])):
        high, low = split(value)
        fac[n, 0] = high
        fac[n, 1] = low

    sib = (r, col(y, z, 1 - q))

    @pl.when(yl != y)
    def _():
        pt_copy().wait_recv()

    dt = remote(tr.at[q], tr.at[q], dt_s, dt_r, sib)
    dt.start()

    def d_copy(k, side):
        part = jr.at[pl.ds((side * 8 + k) * 2, 2)]
        return remote(part, part, d_s.at[k], d_r.at[k], sib)

    @pl.loop(0, 8)
    def _(i):
        k = lax.rem(r + i, 8)

        @pl.when(jnp.logical_not((k == r) & (yl == y)))
        def _():
            p_copy(0, 0, k, 0, (r, c)).wait_recv()
            p_copy(0, 0, k, 1, (r, c)).wait_recv()

        d_copy(k, q).start()

    remote(tr.at[q], tr.at[1 - q], dt_s, dt_r, sib).wait_recv()
    tab_copy = pltpu.make_async_copy(tr, table, tab_sem)
    tab_copy.start()
    tab_copy.wait()

    @pl.loop(0, 8)
    def _(k):
        d_copy(k, 1 - q).wait_recv()


    def dense(k):
        for bb in range(2):
            for qq in range(2):
                for l in range(4):
                    at = table[qq, bb, k, l]
                    at = jnp.where(at < 8, (qq * 8 + at) * 2 + bb, 32)
                    place = ((2 * bb + qq) * 4 + l) * 128
                    lhs[k, :, place:place + 128] = jr[at]

    cov_copy.wait()

    def r_copy(g, k):
        return remote(psend.at[g, k], rbuf.at[g, r], r_s.at[g, k], r_r.at[g, r], (k, c))

    for g in range(2):

        @pl.loop(0, 4)
        def _(i):
            pair = lax.rem(r // 2 + 1 + i, 4)
            if g == 0:
                dense(2 * pair)
                dense(2 * pair + 1)
            part = dot(
                lhs[pl.ds(2 * pair, 2)].reshape(256, 2048), cov[:, g * 256:(g + 1) * 256]
            )
            for h in range(2):
                k = 2 * pair + h

                @pl.when(k == r)
                def _():
                    pown[g] = part[h * 128:(h + 1) * 128]

                @pl.when(k != r)
                def _():
                    psend[g, k] = part[h * 128:(h + 1) * 128].astype(BF16)
                    if g == 0:
                        r_copy(g, k).start()

    @pl.loop(1, 8)
    def _(i):
        r_copy(0, lax.rem(r + i, 8)).wait_send()

    @pl.loop(1, 8)
    def _(i):
        r_copy(1, lax.rem(r + i, 8)).start()


    def block(zz, qq):
        return pl.ds((lax.rem(zz, 4) * 2 + qq) * 4, 4)

    def half(zz, qq, yy):
        return pl.ds(((lax.rem(zz, 4) * 2 + qq) * 2 + yy) * 2, 2)

    def strip(a):
        return pl.ds(pl.multiple_of(a * 128, 128), 128)

    def a_copy(g, i, dev):
        return remote(
            xt.at[g, lax.rem(i, 2)], xz.at[g, z // 2], a_s.at[g, i], a_r.at[g, z // 2], dev
        )

    def b_copy(g, n, yy, dev):
        return remote(
            xz.at[g, n], xb.at[g, block(z, q), :, strip(r)],
            b_s.at[g, n, yy], b_r.at[g, r], dev,
        )

    def y_copy(g, k):
        return remote(yb.at[g, r], yb.at[g, r], y_s.at[g, k], y_r.at[g, r], (k, c))

    def total(g):
        @pl.loop(1, 8)
        def _(i):
            k = lax.rem(r + 8 - i, 8)
            remote(psend.at[g, 0], rbuf.at[g, k], r_s.at[g, 0], r_r.at[g, k], (r, c)).wait_recv()
            pown[g] += rbuf[g, k].astype(F32)

        mine = pown[g]
        yb[g, r] = mine.astype(BF16)
        turned = mine.T.astype(BF16).reshape(2, 4, 32, 128)
        for i in range(4):
            for yy in range(2):
                xt[g, i % 2, yy * 2 + i // 2] = turned[yy, i]
        xz[g, z // 2] = xt[g, (z // 2) % 2]

        for n in range(1, 4):
            i = lax.rem(z // 2 + n, 4)
            a_copy(g, i, (r, col(y, i * 2 + z % 2, q))).start()

    def turn(g):
        for n_ in range(4):
            n = lax.rem(z // 2 + (0, 1, 3, 2)[n_], 4)
            if n_ > 0:
                remote(xt.at[g, 0], xz.at[g, n], a_s.at[g, 0], a_r.at[g, n], (r, c)).wait_recv()
            to = 4 * y + n
            for yy in range(2):
                here = (to == r) & (yy == y)

                @pl.when(jnp.logical_not(here))
                def _():
                    b_copy(g, n, yy, (to, col(yy, z, q))).start()

                @pl.when(here)
                def _():
                    xb[g, block(z, q), :, strip(r)] = xz[g, n]

    def to_rows(g):
        @pl.loop(1, 8)
        def _(i):
            y_copy(g, lax.rem(r + i, 8)).start()

    def fwd(g, zz, qq, yy, sems_s, sems_r, n, dev):
        part = xb.at[g, half(zz, qq, yy)]
        return remote(part, part, sems_s.at[g, n], sems_r.at[g, n], dev)

    up = (r, col(y, lax.rem(z + 1, 8), q))
    down = (r, col(y, lax.rem(z + 7, 8), q))

    def go_up(g, d, yy):
        return fwd(g, z + 4 - d, q, yy, u_s, u_r, d * 2 + yy, up)

    def go_down(g, d, yy):
        return fwd(g, z + d, q, yy, v_s, v_r, d * 2 + yy, down)

    def over(g, d, yy, qq):
        return fwd(g, z + d, qq, yy, s_s, s_r, d * 2 + yy, sib)

    def held(g):
        @pl.loop(0, 8)
        def _(a):
            @pl.when(jnp.logical_not((a == r) & (yl == y)))
            def _():
                remote(
                    xz.at[g, 0], xb.at[g, block(z, q), :, strip(a)],
                    b_s.at[g, 0, 0], b_r.at[g, a], (r, c),
                ).wait_recv()

        go_up(g, 0, 0).start()
        go_down(g, 0, 1).start()
        go_up(g, 0, 1).start()
        go_down(g, 0, 0).start()
        over(g, 0, 0, q).start()
        over(g, 0, 1, q).start()

    def came_up(g, d, yy):
        fwd(g, z + 4 - d, q, yy, u_s, u_r, (d - 1) * 2 + yy, up).wait_recv()

    def came_down(g, d, yy):
        fwd(g, z + d, q, yy, v_s, v_r, (d - 1) * 2 + yy, down).wait_recv()

    def ring1(g):
        came_up(g, 1, 0)
        go_up(g, 1, 0).start()
        over(g, 3, 0, q).start()
        came_down(g, 1, 1)
        go_down(g, 1, 1).start()
        over(g, 1, 1, q).start()

    def ring2(g):
        came_up(g, 1, 1)
        over(g, 3, 1, q).start()
        came_down(g, 1, 0)
        over(g, 1, 0, q).start()

    def ring3(g):
        came_up(g, 2, 0)
        over(g, 2, 0, q).start()
        came_down(g, 2, 1)
        over(g, 2, 1, q).start()

    def solve(g):
        @pl.loop(1, 8)
        def _(i):
            k = lax.rem(r + 8 - i, 8)
            remote(yb.at[g, r], yb.at[g, k], y_s.at[g, 0], y_r.at[g, k], (r, c)).wait_recv()

        cut = pl.ds(g * 256, 256)
        y1 = yb[g, 0:4].reshape(512, 256)
        y2 = yb[g, 4:8].reshape(512, 256)
        z2 = y2.astype(F32) - (dot(fac[0, 0], y1) + dot(fac[0, 1], y1))
        zh, zl = split(z2)
        w1 = dot(fac[2, 0], y1) + dot(fac[2, 1], y1)
        w2 = dot(fac[3, 0], zh) + dot(fac[3, 1], zh) + dot(fac[3, 0], zl)
        wh, wl = split(w2)
        top = w1 - (dot(fac[1, 0], wh) + dot(fac[1, 1], wh) + dot(fac[1, 0], wl))
        wb[pl.ds(0, 512), cut] = top.astype(BF16)
        wb[pl.ds(512, 512), cut] = wh

    def finish(g, off):
        for yy in range(2):
            over(g, off, yy, 1 - q).wait_recv()

        zz = lax.rem(z + off, 4)
        x8 = xb[g, pl.ds(zz * 8, 8)].reshape(256, 1024)
        delta = dot(x8, wb[...])
        for qq in range(2):
            for yy in range(2):
                for m in range(2):
                    row = ((zz % 2) * 2 + qq) * 512 + g * 256 + (yy * 4 + m * 2 + zz // 2) * 32
                    rows = pl.ds(pl.multiple_of(row, 32), 32)
                    n = ((qq * 2 + yy) * 2 + m) * 32
                    ob[rows, :] = (cov[rows, :].astype(F32) - delta[n:n + 32]).astype(BF16)

    def out_copy(g, n):
        rows = pl.ds(n * 512 + g * 256, 256)
        return pltpu.make_async_copy(ob.at[rows], out.at[rows], out_sem.at[g, n])

    def store(g):
        for n in range(4):
            out_copy(g, n).start()

    total(0)
    turn(0)
    total(1)
    to_rows(0)
    held(0)
    turn(1)
    ring1(0)
    held(1)
    to_rows(1)
    ring2(0)
    ring3(0)
    solve(0)
    ring1(1)
    solve(1)
    ring2(1)
    for off in range(4):
        finish(0, off)
    store(0)
    finish(1, 0)
    ring3(1)
    for off in (1, 3, 2):
        finish(1, off)
    store(1)

    @pl.loop(1, 8)
    def _(i):
        z_copy(0, i).wait_send()

        @pl.when(tables)
        def _():
            zt_copy(0, i).wait_send()

    for g in range(2):

        @pl.loop(1, 8)
        def _(i):
            k = lax.rem(r + i, 8)
            if g == 1:
                r_copy(g, k).wait_send()
            y_copy(g, k).wait_send()

        for n in range(1, 4):
            a_copy(g, lax.rem(z // 2 + n, 4), (r, c)).wait_send()

        @pl.loop(0, 4)
        def _(n):
            for yy in range(2):

                @pl.when(jnp.logical_not((4 * y + n == r) & (yy == y)))
                def _():
                    b_copy(g, n, yy, (r, c)).wait_send()

        for d in range(4):
            for yy in range(2):
                over(g, d, yy, q).wait_send()
        for d, yy in ((0, 0), (0, 1), (1, 0)):
            go_up(g, d, yy).wait_send()
            go_down(g, d, yy if d == 0 else 1).wait_send()

        for n in range(4):
            out_copy(g, n).wait()

    @pl.loop(0, 8)
    def _(i):
        zz = lax.rem(z + jnp.where(i == 0, 0, near(i)), 8)
        for yy in range(2):

            @pl.when(jnp.logical_not((4 * y + zz // 2 == r) & (y == yy)))
            def _():
                p_copy(i, yy, r, zz, (r, c)).wait_send()

        d_copy(i, q).wait_send()

    @pl.when(yl == y)
    def _():
        pt_copy().wait_send()

    dt.wait_send()


def body(cov, jac_blocks, block_positions, block_counts, lower_cross_block, pivot_inverse):
    dma = pltpu.SemaphoreType.DMA
    vmem = pltpu.VMEM
    h_spec = pl.BlockSpec(memory_space=pltpu.HBM)
    a_spec = pl.BlockSpec(memory_space=pl.ANY)
    s_spec = pl.BlockSpec(memory_space=pltpu.SMEM)
    return pl.pallas_call(
        kernel,
        out_shape=jax.ShapeDtypeStruct(cov.shape, cov.dtype),
        in_specs=[h_spec, s_spec, s_spec, h_spec, h_spec, h_spec],
        out_specs=a_spec,
        scratch_shapes=[
            vmem((2048, 512), BF16),
            vmem((2048, 512), BF16),
            vmem((512, 512), F32),
            vmem((2, 512, 512), F32),
            vmem((8, 128, 128), BF16),
            vmem((8, 8, 128), jnp.int32),
            vmem((33, 128, 128), BF16),
            vmem((2, 2, 8, 128), jnp.int32),
            pltpu.SMEM((2, 2, 8, 128), jnp.int32),
            vmem((8, 128, 2048), BF16),
            vmem((2, 8, 128, 256), BF16),
            vmem((2, 128, 256), F32),
            vmem((2, 8, 128, 256), BF16),
            vmem((2, 8, 128, 256), BF16),
            vmem((2, 2, 4, 32, 128), BF16),
            vmem((2, 4, 4, 32, 128), BF16),
            vmem((2, 32, 32, 1024), BF16),
            vmem((4, 2, 512, 512), BF16),
            vmem((1024, 512), BF16),
            dma, dma, dma, dma, dma, dma((2, 4)),
            dma((8,)), dma((8,)), dma((8,)), dma((8,)),
            dma((8, 2)), dma((8, 2)), dma, dma,
            dma((8,)), dma((8,)), dma, dma,
            dma((2, 8)), dma((2, 8)), dma((2, 8)), dma((2, 8)),
            dma((2, 4)), dma((2, 4)), dma((2, 4, 2)), dma((2, 8)),
            dma((2, 8)), dma((2, 8)),
            dma((2, 4)), dma((2, 4)), dma((2, 4)), dma((2, 4)),
        ],
        compiler_params=pltpu.CompilerParams(
            collective_id=0, has_side_effects=True, vmem_limit_bytes=62 * 1024 * 1024
        ),
        cost_estimate=pl.CostEstimate(flops=9 * 2**30, bytes_accessed=8 * 2**20, transcendentals=0),
    )(jac_blocks, block_positions.T, block_counts, cov, lower_cross_block, pivot_inverse)


def solution(mesh):
    return jax.shard_map(
        body,
        mesh=mesh,
        in_specs=(P("row", "col"), P("col", None, None), P("col", None), P("col"), P(), P()),
        out_specs=P("row", "col"),
        check_vma=False,
    )
```

```python
import jax
import jax.numpy as jnp
from jax import lax
from jax.experimental import pallas as pl
from jax.experimental.pallas import tpu as pltpu
from jax.sharding import PartitionSpec as P

MESH = pl.DeviceIdType.MESH
F32 = jnp.float32
BF16 = jnp.bfloat16


def dot(a, b):
    return jnp.dot(a, b, preferred_element_type=F32)


def split(values):
    high = values.astype(BF16)
    return high, (values - high.astype(F32)).astype(BF16)


def kernel(
    jac, pos, cnt, cov_hbm, lower_hbm, pivot_hbm, out,
    cov, ob, lower, pivot, jz, tz, jr, tr, table, lhs, psend, pown, rbuf, yb, xt, xz, xb, fac, wb,
    cov_sem, low_sem, piv_sem, own_sem, tab_sem, out_sem,
    z_s, z_r, zt_s, zt_r, p_s, p_r, pt_s, pt_r, d_s, d_r, dt_s, dt_r,
    r_s, r_r, y_s, y_r, a_s, a_r, b_s, b_r, s_s, s_r, u_s, u_r, v_s, v_r,
):
    r = lax.axis_index("row")
    c = lax.axis_index("col")
    y = c // 16
    z = (c // 2) % 8
    q = c % 2
    yl = r // 4
    x = r % 4
    b = c // 4
    j = c % 4

    def col(y_, z_, q_):
        return (y_ * 8 + z_) * 2 + q_

    def remote(src, dst, ss, rs, dev):
        return pltpu.make_async_remote_copy(
            src_ref=src, dst_ref=dst, send_sem=ss, recv_sem=rs, device_id=dev, device_id_type=MESH
        )

    low_copy = pltpu.make_async_copy(lower_hbm, lower, low_sem)
    piv_copy = pltpu.make_async_copy(pivot_hbm, pivot, piv_sem)
    cov_copy = pltpu.make_async_copy(cov_hbm, cov, cov_sem)
    own_copy = pltpu.make_async_copy(jac.at[r], jz.at[z], own_sem)
    own_copy.start()
    low_copy.start()
    piv_copy.start()
    cov_copy.start()

    barrier = pltpu.get_barrier_semaphore()

    def ready(row, col_):
        pl.semaphore_signal(barrier, inc=1, device_id=(row, col_), device_id_type=MESH)

    @pl.loop(1, 8)
    def _(i):
        ready(r, col(y, lax.rem(z + i, 8), q))

    @pl.loop(0, 8)
    def _(a):
        @pl.when(jnp.logical_not((a == r) & (yl == y)))
        def _():
            ready(a, col(yl, z, q))

    ready(r, col(y, z, 1 - q))

    sub = lax.broadcasted_iota(jnp.int32, (8, 128), 0)
    lane = lax.broadcasted_iota(jnp.int32, (8, 128), 1)
    t = jnp.full((8, 128), 8, jnp.int32)
    for s in range(8):
        hit = (sub == pos[0, s]) & (lane == pos[1, s] - c * 4) & (s < cnt[0])
        t = jnp.where(hit, s, t)
    tz[z] = t
    pl.semaphore_wait(barrier, jnp.where(yl == y, 15, 16))

    def z_copy(zz, i):
        return remote(jac.at[r], jz.at[z], z_s.at[i], z_r.at[z], (r, col(y, zz, q)))

    def zt_copy(zz, i):
        return remote(tz.at[z], tz.at[z], zt_s.at[i], zt_r.at[z], (r, col(y, zz, q)))

    tables = (yl == y) & (z // 2 == x)

    def near(i):
        return jnp.where(i % 2 == 1, (i + 1) // 2, 8 - i // 2)

    @pl.loop(1, 8)
    def _(i):
        zz = lax.rem(z + near(i), 8)
        z_copy(zz, i).start()

        @pl.when(tables)
        def _():
            zt_copy(zz, i).start()

    jr[32] = jnp.zeros((128, 128), BF16)
    own_copy.wait()

    def p_copy(i, yy, k, zz, dev):
        return remote(
            jz.at[zz], jr.at[(q * 8 + k) * 2 + zz % 2], p_s.at[i, yy], p_r.at[k, zz % 2], dev
        )

    @pl.loop(0, 8)
    def _(i):
        zz = lax.rem(z + jnp.where(i == 0, 0, near(i)), 8)
        to = 4 * y + zz // 2

        @pl.when(i != 0)
        def _():
            remote(jac.at[r], jz.at[zz], z_s.at[0], z_r.at[zz], (r, c)).wait_recv()

            @pl.when(to == r)
            def _():
                remote(tz.at[zz], tz.at[zz], zt_s.at[0], zt_r.at[zz], (r, c)).wait_recv()

        @pl.when(jnp.logical_not((to == r) & (y == 0)))
        def _():
            p_copy(i, 0, r, zz, (to, col(0, z, q))).start()

        @pl.when(jnp.logical_not((to == r) & (y == 1)))
        def _():
            p_copy(i, 1, r, zz, (to, col(1, z, q))).start()

        @pl.when(to == r)
        def _():
            jr[(q * 8 + r) * 2 + zz % 2] = jz[zz]
            tr[q, zz % 2] = tz[zz]

    def pt_copy():
        return remote(
            tr.at[q], tr.at[q], pt_s, pt_r, (r, col(1 - y, z, q))
        )

    @pl.when(yl == y)
    def _():
        pt_copy().start()

    low_copy.wait()
    piv_copy.wait()
    for n, value in enumerate((lower[...], lower[...].T, pivot[0], pivot[1])):
        high, low = split(value)
        fac[n, 0] = high
        fac[n, 1] = low

    sib = (r, col(y, z, 1 - q))

    @pl.when(yl != y)
    def _():
        pt_copy().wait_recv()

    dt = remote(tr.at[q], tr.at[q], dt_s, dt_r, sib)
    dt.start()

    def d_copy(k, side):
        part = jr.at[pl.ds((side * 8 + k) * 2, 2)]
        return remote(part, part, d_s.at[k], d_r.at[k], sib)

    @pl.loop(0, 8)
    def _(i):
        k = lax.rem(r + i, 8)

        @pl.when(jnp.logical_not((k == r) & (yl == y)))
        def _():
            p_copy(0, 0, k, 0, (r, c)).wait_recv()
            p_copy(0, 0, k, 1, (r, c)).wait_recv()

        d_copy(k, q).start()

    remote(tr.at[q], tr.at[1 - q], dt_s, dt_r, sib).wait_recv()
    tab_copy = pltpu.make_async_copy(tr, table, tab_sem)
    tab_copy.start()
    tab_copy.wait()

    @pl.loop(0, 8)
    def _(k):
        d_copy(k, 1 - q).wait_recv()


    def dense(k):
        for bb in range(2):
            for qq in range(2):
                for l in range(4):
                    at = table[qq, bb, k, l]
                    at = jnp.where(at < 8, (qq * 8 + at) * 2 + bb, 32)
                    place = ((2 * bb + qq) * 4 + l) * 128
                    lhs[k, :, place:place + 128] = jr[at]

    cov_copy.wait()

    def r_copy(g, k):
        return remote(psend.at[g, k], rbuf.at[g, r], r_s.at[g, k], r_r.at[g, r], (k, c))

    for g in range(2):

        @pl.loop(0, 4)
        def _(i):
            pair = lax.rem(r // 2 + 1 + i, 4)
            if g == 0:
                dense(2 * pair)
                dense(2 * pair + 1)
            part = dot(
                lhs[pl.ds(2 * pair, 2)].reshape(256, 2048), cov[:, g * 256:(g + 1) * 256]
            )
            for h in range(2):
                k = 2 * pair + h

                @pl.when(k == r)
                def _():
                    pown[g] = part[h * 128:(h + 1) * 128]

                @pl.when(k != r)
                def _():
                    psend[g, k] = part[h * 128:(h + 1) * 128].astype(BF16)
                    if g == 0:
                        r_copy(g, k).start()

    @pl.loop(1, 8)
    def _(i):
        r_copy(0, lax.rem(r + i, 8)).wait_send()

    @pl.loop(1, 8)
    def _(i):
        r_copy(1, lax.rem(r + i, 8)).start()


    def block(zz, qq):
        return pl.ds((lax.rem(zz, 4) * 2 + qq) * 4, 4)

    def half(zz, qq, yy):
        return pl.ds(((lax.rem(zz, 4) * 2 + qq) * 2 + yy) * 2, 2)

    def strip(a):
        return pl.ds(pl.multiple_of(a * 128, 128), 128)

    def a_copy(g, i, dev):
        return remote(
            xt.at[g, lax.rem(i, 2)], xz.at[g, z // 2], a_s.at[g, i], a_r.at[g, z // 2], dev
        )

    def b_copy(g, n, yy, dev):
        return remote(
            xz.at[g, n], xb.at[g, block(z, q), :, strip(r)],
            b_s.at[g, n, yy], b_r.at[g, r], dev,
        )

    def y_copy(g, k):
        return remote(yb.at[g, r], yb.at[g, r], y_s.at[g, k], y_r.at[g, r], (k, c))

    def total(g):
        @pl.loop(1, 8)
        def _(i):
            k = lax.rem(r + 8 - i, 8)
            remote(psend.at[g, 0], rbuf.at[g, k], r_s.at[g, 0], r_r.at[g, k], (r, c)).wait_recv()
            pown[g] += rbuf[g, k].astype(F32)

        mine = pown[g]
        yb[g, r] = mine.astype(BF16)
        turned = mine.T.astype(BF16).reshape(2, 4, 32, 128)
        for i in range(4):
            for yy in range(2):
                xt[g, i % 2, yy * 2 + i // 2] = turned[yy, i]
        xz[g, z // 2] = xt[g, (z // 2) % 2]

        for n in range(1, 4):
            i = lax.rem(z // 2 + n, 4)
            a_copy(g, i, (r, col(y, i * 2 + z % 2, q))).start()

    def turn(g):
        for n_ in range(4):
            n = lax.rem(z // 2 + (0, 1, 3, 2)[n_], 4)
            if n_ > 0:
                remote(xt.at[g, 0], xz.at[g, n], a_s.at[g, 0], a_r.at[g, n], (r, c)).wait_recv()
            to = 4 * y + n
            for yy in range(2):
                here = (to == r) & (yy == y)

                @pl.when(jnp.logical_not(here))
                def _():
                    b_copy(g, n, yy, (to, col(yy, z, q))).start()

                @pl.when(here)
                def _():
                    xb[g, block(z, q), :, strip(r)] = xz[g, n]

    def to_rows(g):
        @pl.loop(1, 8)
        def _(i):
            y_copy(g, lax.rem(r + i, 8)).start()

    def fwd(g, zz, qq, yy, sems_s, sems_r, n, dev):
        part = xb.at[g, half(zz, qq, yy)]
        return remote(part, part, sems_s.at[g, n], sems_r.at[g, n], dev)

    up = (r, col(y, lax.rem(z + 1, 8), q))
    down = (r, col(y, lax.rem(z + 7, 8), q))

    def go_up(g, d, yy):
        return fwd(g, z + 4 - d, q, yy, u_s, u_r, d * 2 + yy, up)

    def go_down(g, d, yy):
        return fwd(g, z + d, q, yy, v_s, v_r, d * 2 + yy, down)

    def over(g, d, yy, qq):
        return fwd(g, z + d, qq, yy, s_s, s_r, d * 2 + yy, sib)

    def held(g):
        @pl.loop(0, 8)
        def _(a):
            @pl.when(jnp.logical_not((a == r) & (yl == y)))
            def _():
                remote(
                    xz.at[g, 0], xb.at[g, block(z, q), :, strip(a)],
                    b_s.at[g, 0, 0], b_r.at[g, a], (r, c),
                ).wait_recv()

        go_up(g, 0, 0).start()
        go_down(g, 0, 1).start()
        go_up(g, 0, 1).start()
        go_down(g, 0, 0).start()
        over(g, 0, 0, q).start()
        over(g, 0, 1, q).start()

    def came_up(g, d, yy):
        fwd(g, z + 4 - d, q, yy, u_s, u_r, (d - 1) * 2 + yy, up).wait_recv()

    def came_down(g, d, yy):
        fwd(g, z + d, q, yy, v_s, v_r, (d - 1) * 2 + yy, down).wait_recv()

    def ring1(g):
        came_up(g, 1, 0)
        go_up(g, 1, 0).start()
        over(g, 3, 0, q).start()
        came_down(g, 1, 1)
        go_down(g, 1, 1).start()
        over(g, 1, 1, q).start()

    def ring2(g):
        came_up(g, 1, 1)
        over(g, 3, 1, q).start()
        came_down(g, 1, 0)
        over(g, 1, 0, q).start()

    def ring3(g):
        came_up(g, 2, 0)
        over(g, 2, 0, q).start()
        came_down(g, 2, 1)
        over(g, 2, 1, q).start()

    def solve(g):
        @pl.loop(1, 8)
        def _(i):
            k = lax.rem(r + 8 - i, 8)
            remote(yb.at[g, r], yb.at[g, k], y_s.at[g, 0], y_r.at[g, k], (r, c)).wait_recv()

        cut = pl.ds(g * 256, 256)
        y1 = yb[g, 0:4].reshape(512, 256)
        y2 = yb[g, 4:8].reshape(512, 256)
        z2 = y2.astype(F32) - (dot(fac[0, 0], y1) + dot(fac[0, 1], y1))
        zh, zl = split(z2)
        w1 = dot(fac[2, 0], y1) + dot(fac[2, 1], y1)
        w2 = dot(fac[3, 0], zh) + dot(fac[3, 1], zh) + dot(fac[3, 0], zl)
        wh, wl = split(w2)
        top = w1 - (dot(fac[1, 0], wh) + dot(fac[1, 1], wh) + dot(fac[1, 0], wl))
        wb[pl.ds(0, 512), cut] = top.astype(BF16)
        wb[pl.ds(512, 512), cut] = wh

    def finish(g, off):
        for yy in range(2):
            over(g, off, yy, 1 - q).wait_recv()

        zz = lax.rem(z + off, 4)
        x8 = xb[g, pl.ds(zz * 8, 8)].reshape(256, 1024)
        delta = dot(x8, wb[...])
        for qq in range(2):
            for yy in range(2):
                for m in range(2):
                    row = ((zz % 2) * 2 + qq) * 512 + g * 256 + (yy * 4 + m * 2 + zz // 2) * 32
                    rows = pl.ds(pl.multiple_of(row, 32), 32)
                    n = ((qq * 2 + yy) * 2 + m) * 32
                    ob[rows, :] = (cov[rows, :].astype(F32) - delta[n:n + 32]).astype(BF16)

    def out_copy(g, n):
        rows = pl.ds(pl.multiple_of(n * 512 + g * 256, 256), 256)
        return pltpu.make_async_copy(ob.at[rows], out.at[rows], out_sem.at[g, n])

    def store(g):
        for n in range(4):
            out_copy(g, n).start()

    total(0)
    turn(0)
    total(1)
    to_rows(0)
    held(0)
    turn(1)
    ring1(0)
    held(1)
    to_rows(1)
    ring2(0)
    ring3(0)
    solve(0)
    ring1(1)
    solve(1)
    ring2(1)
    for off in range(4):
        finish(0, off)
    store(0)
    finish(1, 0)
    ring3(1)
    for off in (1, 3):
        finish(1, off)
    for qq in range(2):
        out_copy(1, lax.rem(z + 1, 2) * 2 + qq).start()
    finish(1, 2)
    for qq in range(2):
        out_copy(1, lax.rem(z, 2) * 2 + qq).start()

    @pl.loop(1, 8)
    def _(i):
        z_copy(0, i).wait_send()

        @pl.when(tables)
        def _():
            zt_copy(0, i).wait_send()

    for g in range(2):

        @pl.loop(1, 8)
        def _(i):
            k = lax.rem(r + i, 8)
            if g == 1:
                r_copy(g, k).wait_send()
            y_copy(g, k).wait_send()

        for n in range(1, 4):
            a_copy(g, lax.rem(z // 2 + n, 4), (r, c)).wait_send()

        @pl.loop(0, 4)
        def _(n):
            for yy in range(2):

                @pl.when(jnp.logical_not((4 * y + n == r) & (yy == y)))
                def _():
                    b_copy(g, n, yy, (r, c)).wait_send()

        for d in range(4):
            for yy in range(2):
                over(g, d, yy, q).wait_send()
        for d, yy in ((0, 0), (0, 1), (1, 0)):
            go_up(g, d, yy).wait_send()
            go_down(g, d, yy if d == 0 else 1).wait_send()

        for n in range(4):
            out_copy(g, n).wait()

    @pl.loop(0, 8)
    def _(i):
        zz = lax.rem(z + jnp.where(i == 0, 0, near(i)), 8)
        for yy in range(2):

            @pl.when(jnp.logical_not((4 * y + zz // 2 == r) & (y == yy)))
            def _():
                p_copy(i, yy, r, zz, (r, c)).wait_send()

        d_copy(i, q).wait_send()

    @pl.when(yl == y)
    def _():
        pt_copy().wait_send()

    dt.wait_send()


def body(cov, jac_blocks, block_positions, block_counts, lower_cross_block, pivot_inverse):
    dma = pltpu.SemaphoreType.DMA
    vmem = pltpu.VMEM
    h_spec = pl.BlockSpec(memory_space=pltpu.HBM)
    a_spec = pl.BlockSpec(memory_space=pl.ANY)
    s_spec = pl.BlockSpec(memory_space=pltpu.SMEM)
    return pl.pallas_call(
        kernel,
        out_shape=jax.ShapeDtypeStruct(cov.shape, cov.dtype),
        in_specs=[h_spec, s_spec, s_spec, h_spec, h_spec, h_spec],
        out_specs=a_spec,
        scratch_shapes=[
            vmem((2048, 512), BF16),
            vmem((2048, 512), BF16),
            vmem((512, 512), F32),
            vmem((2, 512, 512), F32),
            vmem((8, 128, 128), BF16),
            vmem((8, 8, 128), jnp.int32),
            vmem((33, 128, 128), BF16),
            vmem((2, 2, 8, 128), jnp.int32),
            pltpu.SMEM((2, 2, 8, 128), jnp.int32),
            vmem((8, 128, 2048), BF16),
            vmem((2, 8, 128, 256), BF16),
            vmem((2, 128, 256), F32),
            vmem((2, 8, 128, 256), BF16),
            vmem((2, 8, 128, 256), BF16),
            vmem((2, 2, 4, 32, 128), BF16),
            vmem((2, 4, 4, 32, 128), BF16),
            vmem((2, 32, 32, 1024), BF16),
            vmem((4, 2, 512, 512), BF16),
            vmem((1024, 512), BF16),
            dma, dma, dma, dma, dma, dma((2, 4)),
            dma((8,)), dma((8,)), dma((8,)), dma((8,)),
            dma((8, 2)), dma((8, 2)), dma, dma,
            dma((8,)), dma((8,)), dma, dma,
            dma((2, 8)), dma((2, 8)), dma((2, 8)), dma((2, 8)),
            dma((2, 4)), dma((2, 4)), dma((2, 4, 2)), dma((2, 8)),
            dma((2, 8)), dma((2, 8)),
            dma((2, 4)), dma((2, 4)), dma((2, 4)), dma((2, 4)),
        ],
        compiler_params=pltpu.CompilerParams(
            collective_id=0, has_side_effects=True, vmem_limit_bytes=62 * 1024 * 1024
        ),
        cost_estimate=pl.CostEstimate(flops=9 * 2**30, bytes_accessed=8 * 2**20, transcendentals=0),
    )(jac_blocks, block_positions.T, block_counts, cov, lower_cross_block, pivot_inverse)


def solution(mesh):
    return jax.shard_map(
        body,
        mesh=mesh,
        in_specs=(P("row", "col"), P("col", None, None), P("col", None), P("col"), P(), P()),
        out_specs=P("row", "col"),
        check_vma=False,
    )
```
